32 devices in a mesh: img: 2 (over y), dp: 16 (over z, x, core).
Axes of the slice: x: 2, y: 2, z: 4, core: 2. Of those that a mesh axis runs over, the one named last changes fastest.
Arguments:
- inputs: float32 [16, 768, 1152], P('dp', 'img'), may hold values from -16 to 16
- flat_params: bfloat16 [15253504], P(('img', 'dp')), may hold values from -2.5 to 2.5
- bias_table: bfloat16 [2816, 16], P(('img', 'dp')), may hold values from -1 to 252
- bucket_index: int32 [768, 768], replicated, may hold values from 0 to 2815, as said below
- valid_mask: int32 [16, 768], P('dp'), may hold values 0 or 1
- cotangent: float32 [16, 768, 1152], P('dp', 'img'), may hold values from -6 to 6
Outputs:
- layer_out: float32 [16, 768, 1152], P('dp', 'img')
- grad_inputs: float32 [16, 768, 1152], P('dp', 'img')
- grad_params: float32 [15253504], P(('img', 'dp'))
- grad_vectors: float32 [16384], P(('img', 'dp'))
- grad_table: float32 [2816, 16], P(('img', 'dp'))
The draws below stay inside these ranges and needn't reach their ends.
Inputs may be any that keep to these rules, and one draw needn't show every extreme that they name: `bucket_index`: entry (i, j) is the bucket (r + 26) * 53 + c + 26 of the row and column offset (r, c) between the grid positions of the patches in token slots i and j on a 27 x 27 grid; every patch stands in one slot; pairs with an empty slot take bucket 2816 - 1.
All inputs are finite; a program needn't handle non-finite values. No bound on the sum of `valid_mask` on one device may be relied on, other than what follows from the above.
Results may differ from the reference program's by a relative error of at most 0.0085.
Values may be sent and summed in bfloat16 or wider, within the bound.
No kernel may reach another device: no remote copies, remote signals or barrier semaphores. Data moves between devices by JAX's collectives and lax.ppermute only.
A program may use at most 704 MiB of HBM per device.

```python
import math
import jax
import jax.numpy as jnp
from jax import lax

D = 1152
FF = 4304
H = 16
DH = 72
SEQ = 768
GRID = 27
NB = 2816
IMAGES = 16
PARAMS_PAD = 15253504
VEC_PAD = 16384


def slot_order(key):
    return jax.random.permutation(key, SEQ).astype(jnp.int32)


def draw_inputs(key, part):
    slot_patch = slot_order(key)
    key = jax.random.fold_in(key, 11)
    noise_key, place_key = jax.random.split(key, 2)
    is_patch = slot_patch < GRID * GRID
    row_frac = (slot_patch // GRID).astype(jnp.float32) / (GRID - 1) - 0.5
    col_frac = (slot_patch % GRID).astype(jnp.float32) / (GRID - 1) - 0.5
    row_frac = jnp.where(is_patch, row_frac, 0.0)
    col_frac = jnp.where(is_patch, col_frac, 0.0)
    directions = jnp.clip(jax.random.normal(place_key, (2, D), jnp.float32), -4.0, 4.0)
    place_part = 4.0 * (row_frac[:, None] * directions[0][None, :] + col_frac[:, None] * directions[1][None, :])
    noise_part = jnp.clip(jax.random.normal(noise_key, (IMAGES, SEQ, D), jnp.float32), -5.0, 5.0)
    values = noise_part + place_part[None, :, :]
    return jnp.clip(values, -16.0, 16.0)


def draw_flat_params(key, part):
    key = jax.random.fold_in(key, 3)
    position = jnp.arange(PARAMS_PAD)
    raw_noise = jnp.clip(jax.random.normal(key, (PARAMS_PAD,), jnp.float32), -5.0, 5.0)
    end_qkv = 3 * D * D
    end_out = end_qkv + D * D
    end_up = end_out + D * FF
    end_down = end_up + FF * D
    gain_one = (position >= end_down) & (position < end_down + D)
    gain_two = (position >= end_down + 5 * D) & (position < end_down + 6 * D)
    is_gain = gain_one | gain_two
    spread_of = jnp.where(is_gain, 0.1, 0.5)
    spread_of = jnp.where(position < end_down, FF ** (-0.5), spread_of)
    spread_of = jnp.where(position < end_up, D ** (-0.5), spread_of)
    spread_of = jnp.where(position < end_out, 8.0 * D ** (-0.5), spread_of)
    spread_of = jnp.where(position < end_qkv, D ** (-0.5), spread_of)
    query_key = (position < end_qkv) & (position % (3 * D) < 2 * D)
    spread_of = jnp.where(query_key, 0.3 * D ** (-0.5), spread_of)
    offset = jnp.where(is_gain, 1.0, 0.0)
    return jnp.clip(offset + spread_of * raw_noise, -2.5, 2.5).astype(jnp.bfloat16)


def draw_bias_table(key, part):
    key = jax.random.fold_in(key, 7)
    span_width = 2 * GRID - 1
    window_reach = 10 * GRID // 27
    bucket_ids = jnp.arange(NB)[:, None]
    rel_row = bucket_ids // span_width - (GRID - 1)
    rel_col = bucket_ids % span_width - (GRID - 1)
    near_mask = (jnp.abs(rel_row) <= window_reach) & (jnp.abs(rel_col) <= window_reach) & (bucket_ids < span_width * span_width)
    near_lift = jnp.where(near_mask, 3.2, 0.0)
    base_draw = near_lift + 0.1 * jnp.clip(jax.random.normal(key, (NB, H), jnp.float32), -5.0, 5.0)
    return base_draw.astype(jnp.bfloat16)


def draw_bucket_index(key, part):
    slot_patch = slot_order(key)
    is_patch = slot_patch < GRID * GRID
    row_place = slot_patch // GRID
    col_place = slot_patch % GRID
    span_width = 2 * GRID - 1
    bucket_ids = (row_place[:, None] - row_place[None, :] + GRID - 1) * span_width + (col_place[:, None] - col_place[None, :] + GRID - 1)
    both_patches = is_patch[:, None] & is_patch[None, :]
    return jnp.where(both_patches, bucket_ids, NB - 1).astype(jnp.int32)


def with_ends(result, rng, low, high):
    longest = result.shape.index(max(result.shape))
    spots = []
    for shift in (0, 1):
        where = [jax.random.randint(jax.random.fold_in(rng, axis), (), 0, length) for axis, length in enumerate(result.shape)]
        where[longest] = (where[longest] + shift) % result.shape[longest]
        spots.append(tuple(where))
    return result.at[spots[0]].set(low).at[spots[1]].set(high)


def block_scale(key, shape, pieces, smallest, top_value):
    factor_of, own = 1.0, jax.random.fold_in(key, 6)
    for dim, shards_of in pieces:
        heights = jnp.exp(jax.random.uniform(jax.random.fold_in(own, dim), (shards_of,), jnp.float32, smallest / len(pieces), top_value / len(pieces)))
        factor_of = factor_of * jnp.repeat(heights, shape[dim] // shards_of).reshape([-1 if axis == dim else 1 for axis in range(len(shape))])
    return factor_of


def gaussian(own_key, dims, spread, bound, pieces=(), kind=jnp.bfloat16):
    array = jax.random.normal(own_key, dims, jnp.float32) * spread
    if len(pieces) > 0:
        array = block_scale(own_key, dims, pieces, -0.22, 0.18) * array
    return jnp.clip(array, min=-bound, max=bound).astype(kind)


def setup_inputs(seed: int = 0) -> dict:
    arg_keys = jax.random.split(jax.random.key(seed), 7)
    return {
        "inputs": draw_inputs(jax.random.fold_in(arg_keys[6], 71), 0),
        "flat_params": draw_flat_params(jax.random.fold_in(arg_keys[6], 71), 0),
        "bias_table": draw_bias_table(jax.random.fold_in(arg_keys[6], 71), 0),
        "bucket_index": draw_bucket_index(jax.random.fold_in(arg_keys[6], 71), 0),
        "valid_mask": with_ends((jax.random.randint(arg_keys[4], (IMAGES, SEQ), 0, 8) < 7).astype(jnp.int32), jax.random.fold_in(arg_keys[4], 1), 0, 1),
        "cotangent": gaussian(arg_keys[5], (IMAGES, SEQ, D), 1.0, 6.0, ((0, 16), (1, 2)), jnp.float32),
    }


EPS = 1e-06
PENALTY = 30000.0
GELU_C = math.sqrt(2.0 / math.pi)
GELU_K = 0.044715

def contract_rows(left_side, right_side):
    return lax.dot_general(left_side, right_side, (((0,), (0,)), ((), ())), preferred_element_type=jnp.float32)

def times_transposed(left_side, right_side):
    return lax.dot_general(left_side, right_side, (((1,), (1,)), ((), ())), preferred_element_type=jnp.float32)

def segment_lengths(model_width, hidden_width):
    return [3 * model_width * model_width, model_width * model_width, model_width * hidden_width, hidden_width * model_width] + [model_width] * 8 + [hidden_width]

def unpack(flat_full, model_width, hidden_width):
    segments = []
    cursor = 0
    for length in segment_lengths(model_width, hidden_width):
        segments.append(flat_full[cursor:cursor + length])
        cursor = cursor + length
    w_qkv = segments[0].reshape(model_width, 3 * model_width)
    w_out = segments[1].reshape(model_width, model_width)
    w_up = segments[2].reshape(model_width, hidden_width)
    w_down = segments[3].reshape(hidden_width, model_width)
    vectors = [segment.astype(jnp.float32) for segment in segments[4:]]
    return (w_qkv, w_out, w_up, w_down, vectors)

def pack(gradients, padded_total):
    flat_grad = jnp.concatenate([grad_piece.reshape(-1) for grad_piece in gradients])
    return jnp.concatenate([flat_grad, jnp.zeros((padded_total - flat_grad.shape[0],), jnp.float32)])

def layer_norm(stream, gain, shift):
    centered = stream - lax.optimization_barrier(jnp.mean(stream, axis=-1, keepdims=True))
    inv_std = lax.rsqrt(lax.optimization_barrier(jnp.mean(centered * centered, axis=-1, keepdims=True)) + EPS)
    normed = centered * inv_std
    return (normed * gain + shift, normed, inv_std)

def norm_back(grad_out, normed, inv_std, gain):
    grad_normed = grad_out * gain
    grad_in = inv_std * (grad_normed - lax.optimization_barrier(jnp.mean(grad_normed, axis=-1, keepdims=True)) - normed * lax.optimization_barrier(jnp.mean(grad_normed * normed, axis=-1, keepdims=True)))
    return (grad_in, lax.optimization_barrier(jnp.sum(grad_out * normed, axis=0)), lax.optimization_barrier(jnp.sum(grad_out, axis=0)))

def gelu_parts(pre_act):
    tanh_val = jnp.tanh(GELU_C * (pre_act + GELU_K * pre_act ** 3))
    activated = 0.5 * pre_act * (1.0 + tanh_val)
    derivative = 0.5 * (1.0 + tanh_val) + 0.5 * pre_act * (1.0 - tanh_val * tanh_val) * GELU_C * (1.0 + 3.0 * GELU_K * pre_act * pre_act)
    return (activated, derivative)

def split_heads(rows_in, head_count):
    return rows_in.reshape(rows_in.shape[0], head_count, -1)

def score_block(query_heads, key_heads, bias_terms, valid_keys):
    head_dim = query_heads.shape[-1]
    logits = jnp.einsum('qhd,khd->hqk', query_heads.astype(jnp.float32), key_heads.astype(jnp.float32))
    penalty_row = PENALTY * (1.0 - valid_keys.astype(jnp.float32))
    return logits * head_dim ** (-0.5) + bias_terms - penalty_row[None, None, :]

def reference(inputs, flat_params, bias_table, bucket_index, valid_mask, cotangent):
    w_qkv, w_out, w_up, w_down, vectors = unpack(flat_params, D, FF)
    norm1_gain, norm1_shift, bias_query, bias_value, bias_out, norm2_gain, norm2_shift, bias_down, bias_up = vectors
    table_heads = bias_table.astype(jnp.float32).T
    bias_terms = jnp.take(table_heads, bucket_index, axis=1)
    flat_buckets = bucket_index.reshape(-1)

    def head_segments(head_scores):
        return jax.ops.segment_sum(head_scores, flat_buckets, num_segments=NB)

    def one_image(carry, image_args):
        stream, valid_keys, grad_out = image_args
        attn_full, normed1, inv_std1 = layer_norm(stream, norm1_gain, norm1_shift)
        attn_in = attn_full.astype(jnp.bfloat16)
        projected = jnp.dot(attn_in, w_qkv, preferred_element_type=jnp.float32)
        query_rows = (projected[:, :D] + bias_query).astype(jnp.bfloat16)
        key_rows = projected[:, D:2 * D].astype(jnp.bfloat16)
        value_rows = (projected[:, 2 * D:] + bias_value).astype(jnp.bfloat16)
        query_heads = split_heads(query_rows, H)
        key_heads = split_heads(key_rows, H)
        value_heads = split_heads(value_rows, H)
        scores = score_block(query_heads, key_heads, bias_terms, valid_keys)
        row_max = lax.optimization_barrier(jnp.max(scores, axis=-1, keepdims=True))
        exp_scores = jnp.exp(scores - row_max)
        row_total = lax.optimization_barrier(jnp.sum(exp_scores, axis=-1, keepdims=True))
        log_norm = row_max + jnp.log(row_total)
        attn_probs = (exp_scores / row_total).astype(jnp.bfloat16)
        attn_heads = jnp.einsum('hqk,khd->qhd', attn_probs.astype(jnp.float32), value_heads.astype(jnp.float32))
        attn_mixed = attn_heads.reshape(SEQ, D).astype(jnp.bfloat16)
        resid = stream + jnp.dot(attn_mixed, w_out, preferred_element_type=jnp.float32) + bias_out
        mlp_full, normed2, inv_std2 = layer_norm(resid, norm2_gain, norm2_shift)
        mlp_in = mlp_full.astype(jnp.bfloat16)
        pre_act = jnp.dot(mlp_in, w_up, preferred_element_type=jnp.float32) + bias_up
        activated, derivative = gelu_parts(pre_act)
        hidden_act = activated.astype(jnp.bfloat16)
        output = resid + jnp.dot(hidden_act, w_down, preferred_element_type=jnp.float32) + bias_down
        grad_out_b = grad_out.astype(jnp.bfloat16)
        g_w_down = contract_rows(hidden_act, grad_out_b)
        g_b_down = lax.optimization_barrier(jnp.sum(grad_out, axis=0))
        grad_pre = times_transposed(grad_out_b, w_down) * derivative
        grad_pre_b = grad_pre.astype(jnp.bfloat16)
        g_w_up = contract_rows(mlp_in, grad_pre_b)
        g_b_up = lax.optimization_barrier(jnp.sum(grad_pre, axis=0))
        resid_part, g_n2_gain, g_n2_shift = norm_back(times_transposed(grad_pre_b, w_up), normed2, inv_std2, norm2_gain)
        grad_resid = grad_out + resid_part
        grad_resid_b = grad_resid.astype(jnp.bfloat16)
        g_w_out = contract_rows(attn_mixed, grad_resid_b)
        g_b_out = lax.optimization_barrier(jnp.sum(grad_resid, axis=0))
        grad_mixed = times_transposed(grad_resid_b, w_out).astype(jnp.bfloat16)
        back_probs = jnp.exp(scores - log_norm)
        grad_heads = split_heads(grad_mixed, H)
        grad_probs = jnp.einsum('qhd,khd->hqk', grad_heads.astype(jnp.float32), value_heads.astype(jnp.float32))
        row_dot = lax.optimization_barrier(jnp.sum(back_probs * grad_probs, axis=-1, keepdims=True))
        grad_scores = back_probs * (grad_probs - row_dot)
        table_part = jax.vmap(head_segments)(grad_scores.reshape(H, -1)).T
        grad_scores_b = grad_scores.astype(jnp.bfloat16).astype(jnp.float32)
        probs_b = back_probs.astype(jnp.bfloat16).astype(jnp.float32)
        scale_factor = DH ** (-0.5)
        grad_query = scale_factor * jnp.einsum('hqk,khd->qhd', grad_scores_b, key_heads.astype(jnp.float32))
        grad_key = scale_factor * jnp.einsum('hqk,qhd->khd', grad_scores_b, query_heads.astype(jnp.float32))
        grad_value = jnp.einsum('hqk,qhd->khd', probs_b, grad_heads.astype(jnp.float32))
        grad_query = grad_query.reshape(SEQ, D)
        grad_key = grad_key.reshape(SEQ, D)
        grad_value = grad_value.reshape(SEQ, D)
        grad_proj_b = jnp.concatenate([grad_query, grad_key, grad_value], axis=-1).astype(jnp.bfloat16)
        g_w_qkv = contract_rows(attn_in, grad_proj_b)
        g_b_query = lax.optimization_barrier(jnp.sum(grad_query, axis=0))
        g_b_value = lax.optimization_barrier(jnp.sum(grad_value, axis=0))
        input_part, g_n1_gain, g_n1_shift = norm_back(times_transposed(grad_proj_b, w_qkv), normed1, inv_std1, norm1_gain)
        grad_in = grad_resid + input_part
        flat_grad = pack([g_w_qkv, g_w_out, g_w_up, g_w_down], PARAMS_PAD)
        vector_grad = pack([g_n1_gain, g_n1_shift, g_b_query, g_b_value, g_b_out, g_n2_gain, g_n2_shift, g_b_down, g_b_up], VEC_PAD)
        return ((carry[0] + flat_grad, carry[1] + vector_grad, carry[2] + table_part), (output, grad_in))
    start_carry = (jnp.zeros((PARAMS_PAD,), jnp.float32), jnp.zeros((VEC_PAD,), jnp.float32), jnp.zeros((NB, H), jnp.float32))
    totals, results = lax.scan(one_image, start_carry, (inputs, valid_mask, cotangent))
    return (results[0], results[1], totals[0], totals[1], totals[2])
```

```python
import math

import jax
import jax.numpy as jnp
from jax import lax
from jax.experimental import pallas as pl
from jax.experimental.pallas import tpu as pltpu
from jax.sharding import PartitionSpec as P

D = 1152
FF = 4304
FFP = 4352
H = 16
HL = 8
DH = 72
SEQ = 768
GRID = 27
SPAN = 53
NB = 2816
PARAMS_PAD = 15253504
VEC_PAD = 16384
EPS = 1e-06
PENALTY = 30000.0
ABSENT = -1e30
GELU_C = math.sqrt(2.0 / math.pi)
GELU_K = 0.044715
SCALE = DH ** (-0.5)

LP = 896
EW = 1792
BF = jnp.bfloat16
F32 = jnp.float32

Q_END = 3 * D * D
O_END = Q_END + D * D
U_END = O_END + D * FF
D_END = U_END + FF * D
VECTORS = 8 * D + FF


def dot(a, b, ca, cb):
    return lax.dot_general(a, b, (((ca,), (cb,)), ((), ())), preferred_element_type=F32)


def offset_of(key_row):
    lead = 26 - key_row
    return lead % 4, (lead // 4) * 128


def wide(column):
    return jnp.concatenate([column] * (LP // 128), axis=1)


def shift_bias(e_ref, e4):
    bias = e_ref[0]
    e4[0] = bias
    for m in range(1, 4):
        e4[m] = pltpu.roll(bias, EW - 32 * m, 1)


def attend_forward(q_ref, k_ref, v_ref, e_ref, pen_ref, out_ref, norm_ref, e4, s_scr, p_scr):
    shift_bias(e_ref, e4)
    q = q_ref[0, 0]
    k = k_ref[0, 0]
    top = jnp.full((32, LP), -jnp.inf, F32)
    for kb in range(7):
        s = dot(k[:, kb * 128 : (kb + 1) * 128], q, 0, 0)
        for sub in range(4):
            row = kb * 4 + sub
            lo = row * 32
            part = s[sub * 32 : sub * 32 + 32] * SCALE
            if row < GRID:
                m, base = offset_of(row)
                part = part + e4[m, :, base : base + LP]
            part = part + wide(pen_ref[lo : lo + 32])
            s_scr[lo : lo + 32] = part
            top = jnp.maximum(top, part)
    row_max = jnp.max(top, axis=0, keepdims=True)
    total = jnp.zeros((32, LP), F32)
    for row in range(28):
        lo = row * 32
        p = jnp.exp(s_scr[lo : lo + 32] - row_max)
        total = total + p
        p_scr[lo : lo + 32] = p.astype(BF)
    row_total = jnp.sum(total, axis=0, keepdims=True)
    mixed = dot(v_ref[0, 0], p_scr[...], 1, 0)
    out_ref[0] = (mixed / row_total).astype(BF)
    norm_ref[0] = row_max + jnp.log(row_total)


def attend_backward(
    q_ref, k_ref, v_ref, do_ref, e_ref, pen_ref, norm_ref,
    grad_ref, acc_ref, sums_ref,
    e4, p_scr, g_scr, pb_scr, gb_scr, acc,
):
    shift_bias(e_ref, e4)
    q = q_ref[0, 0]
    k = k_ref[0, 0]
    v = v_ref[0, 0]
    do = do_ref[0]
    log_norm = norm_ref[0]
    along = jnp.zeros((32, LP), F32)
    for kb in range(7):
        cols = slice(kb * 128, (kb + 1) * 128)
        s = dot(k[:, cols], q, 0, 0)
        g = dot(v[:, cols], do, 0, 0)
        for sub in range(4):
            row = kb * 4 + sub
            lo = row * 32
            part = s[sub * 32 : sub * 32 + 32] * SCALE
            if row < GRID:
                m, base = offset_of(row)
                part = part + e4[m, :, base : base + LP]
            part = part + wide(pen_ref[lo : lo + 32])
            p = jnp.exp(part - log_norm)
            g_part = g[sub * 32 : sub * 32 + 32]
            along = along + p * g_part
            p_scr[lo : lo + 32] = p
            g_scr[lo : lo + 32] = g_part
            pb_scr[lo : lo + 32] = p.astype(BF)
    row_dot = jnp.sum(along, axis=0, keepdims=True)
    acc[...] = jnp.zeros_like(acc)
    for row in range(28):
        lo = row * 32
        ds = p_scr[lo : lo + 32] * (g_scr[lo : lo + 32] - row_dot)
        if row < GRID:
            m, base = offset_of(row)
            acc[m, :, base : base + LP] += ds
        gb_scr[lo : lo + 32] = ds.astype(BF)
    total = acc[0]
    for m in range(1, 4):
        total = total + pltpu.roll(acc[m], 32 * m, 1)
    acc_ref[0] = total
    gb = gb_scr[...]
    dq = dot(k, gb, 1, 0) * SCALE
    dk = dot(q, gb, 1, 1) * SCALE
    dv = dot(do, pb_scr[...], 1, 1)
    grad_ref[0, 0] = dq.astype(BF)
    grad_ref[1, 0] = dk.astype(BF)
    grad_ref[2, 0] = dv.astype(BF)
    sums_ref[0, 0] = jnp.broadcast_to(jnp.sum(dq, axis=1, keepdims=True), (DH, 128))
    sums_ref[1, 0] = jnp.broadcast_to(jnp.sum(dv, axis=1, keepdims=True), (DH, 128))


def head_block(which):
    return pl.BlockSpec((1, 1, DH, LP), lambda h: (which, h, 0, 0))


def run_forward(qkv, bias, pen):
    return pl.pallas_call(
        attend_forward,
        grid=(HL,),
        in_specs=[
            head_block(0),
            head_block(1),
            head_block(2),
            pl.BlockSpec((1, 32, EW), lambda h: (h, 0, 0)),
            pl.BlockSpec((LP, 128), lambda h: (0, 0)),
        ],
        out_specs=[
            pl.BlockSpec((1, DH, LP), lambda h: (h, 0, 0)),
            pl.BlockSpec((1, 1, LP), lambda h: (h, 0, 0)),
        ],
        out_shape=[
            jax.ShapeDtypeStruct((HL, DH, LP), BF),
            jax.ShapeDtypeStruct((HL, 1, LP), F32),
        ],
        scratch_shapes=[
            pltpu.VMEM((4, 32, EW), F32),
            pltpu.VMEM((LP, LP), F32),
            pltpu.VMEM((LP, LP), BF),
        ],
        compiler_params=pltpu.CompilerParams(vmem_limit_bytes=48 * 2**20),
        cost_estimate=pl.CostEstimate(
            flops=HL * 4 * LP * LP * 128, bytes_accessed=8 * 2**20, transcendentals=HL * LP * LP
        ),
        name="attend_forward",
    )(qkv, qkv, qkv, bias, pen)


def run_backward(qkv, d_mixed, bias, pen, log_norm):
    return pl.pallas_call(
        attend_backward,
        grid=(HL,),
        in_specs=[
            head_block(0),
            head_block(1),
            head_block(2),
            pl.BlockSpec((1, DH, LP), lambda h: (h, 0, 0)),
            pl.BlockSpec((1, 32, EW), lambda h: (h, 0, 0)),
            pl.BlockSpec((LP, 128), lambda h: (0, 0)),
            pl.BlockSpec((1, 1, LP), lambda h: (h, 0, 0)),
        ],
        out_specs=[
            pl.BlockSpec((3, 1, DH, LP), lambda h: (0, h, 0, 0)),
            pl.BlockSpec((1, 32, EW), lambda h: (h, 0, 0)),
            pl.BlockSpec((2, 1, DH, 128), lambda h: (0, h, 0, 0)),
        ],
        out_shape=[
            jax.ShapeDtypeStruct((3, HL, DH, LP), BF),
            jax.ShapeDtypeStruct((HL, 32, EW), F32),
            jax.ShapeDtypeStruct((2, HL, DH, 128), F32),
        ],
        scratch_shapes=[
            pltpu.VMEM((4, 32, EW), F32),
            pltpu.VMEM((LP, LP), F32),
            pltpu.VMEM((LP, LP), F32),
            pltpu.VMEM((LP, LP), BF),
            pltpu.VMEM((LP, LP), BF),
            pltpu.VMEM((4, 32, EW), F32),
        ],
        compiler_params=pltpu.CompilerParams(vmem_limit_bytes=48 * 2**20),
        cost_estimate=pl.CostEstimate(
            flops=HL * 10 * LP * LP * 128, bytes_accessed=16 * 2**20, transcendentals=HL * LP * LP
        ),
        name="attend_backward",
    )(qkv, qkv, qkv, d_mixed, bias, pen, log_norm)


FB = 256


def mlp_body(
    x_ref, xt_ref, go_ref, up_ref, down_ref, bias_ref,
    out_ref, gx_ref, g_up_ref, g_down_ref, g_bias_ref,
):
    step = pl.program_id(0)

    @pl.when(step == 0)
    def _():
        out_ref[...] = jnp.zeros_like(out_ref)
        gx_ref[...] = jnp.zeros_like(gx_ref)

    go = go_ref[...]
    up = up_ref[...]
    down = down_ref[...]
    pre = dot(x_ref[...], up, 1, 0) + bias_ref[...]
    square = pre * pre
    t = jnp.tanh(GELU_C * (pre + GELU_K * (square * pre)))
    half = 0.5 * (1.0 + t)
    hidden = (pre * half).astype(BF)
    slope = half + 0.5 * pre * (1.0 - t * t) * (GELU_C * (1.0 + 3.0 * GELU_K * square))
    out_ref[...] += dot(hidden, down, 1, 0)
    g_down_ref[...] = dot(hidden, go, 0, 0).astype(BF)
    grad_pre = dot(go, down, 1, 1) * slope
    g_bias_ref[...] = jnp.sum(grad_pre, axis=0, keepdims=True)
    grad_pre_b = grad_pre.astype(BF)
    g_up_ref[...] = dot(xt_ref[...], grad_pre_b, 1, 0).astype(BF)
    gx_ref[...] += dot(grad_pre_b, up, 1, 1)


def run_mlp(x, grad_out, w_up, w_down, bias_up):
    rows = x.shape[0]
    whole = lambda shape: pl.BlockSpec(shape, lambda j: (0, 0))
    return pl.pallas_call(
        mlp_body,
        grid=(FFP // FB,),
        in_specs=[
            whole((rows, D)),
            whole((D, rows)),
            whole((rows, D)),
            pl.BlockSpec((D, FB), lambda j: (0, j)),
            pl.BlockSpec((FB, D), lambda j: (j, 0)),
            pl.BlockSpec((1, FB), lambda j: (0, j)),
        ],
        out_specs=[
            whole((rows, D)),
            whole((rows, D)),
            pl.BlockSpec((D, FB), lambda j: (0, j)),
            pl.BlockSpec((FB, D), lambda j: (j, 0)),
            pl.BlockSpec((1, FB), lambda j: (0, j)),
        ],
        out_shape=[
            jax.ShapeDtypeStruct((rows, D), F32),
            jax.ShapeDtypeStruct((rows, D), F32),
            jax.ShapeDtypeStruct((D, FFP), BF),
            jax.ShapeDtypeStruct((FFP, D), BF),
            jax.ShapeDtypeStruct((1, FFP), F32),
        ],
        compiler_params=pltpu.CompilerParams(vmem_limit_bytes=48 * 2**20),
        cost_estimate=pl.CostEstimate(
            flops=12 * rows * D * FFP, bytes_accessed=50 * 2**20, transcendentals=rows * FFP
        ),
        name="mlp_both_ways",
    )(x, x.T, grad_out, w_up, w_down, bias_up)


def layer_norm(stream, gain, shift):
    centered = stream - jnp.mean(stream, axis=-1, keepdims=True)
    inv_std = lax.rsqrt(jnp.mean(centered * centered, axis=-1, keepdims=True) + EPS)
    normed = centered * inv_std
    return (normed * gain + shift, normed, inv_std)


def norm_back(grad_out, normed, inv_std, gain):
    grad_normed = grad_out * gain
    grad_in = inv_std * (
        grad_normed
        - jnp.mean(grad_normed, axis=-1, keepdims=True)
        - normed * jnp.mean(grad_normed * normed, axis=-1, keepdims=True)
    )
    return (grad_in, jnp.sum(grad_out * normed, axis=0), jnp.sum(grad_out, axis=0))


def slot_places(bucket_index):
    real = bucket_index < SPAN * SPAN
    row = jnp.max(jnp.where(real, bucket_index // SPAN, -1), axis=1) - (GRID - 1)
    col = jnp.max(jnp.where(real, bucket_index % SPAN, -1), axis=1) - (GRID - 1)
    empty = row < 0
    earlier = jnp.arange(SEQ)[:, None] > jnp.arange(SEQ)[None, :]
    rank = jnp.sum(jnp.where(earlier & empty[None, :], 1, 0), axis=1)
    spare = (rank // 5) * 32 + GRID + rank % 5
    return jnp.where(empty, spare, row * 32 + col)


def column_classes():
    key_col = jnp.arange(1024)[:, None] // 32
    query_col = jnp.arange(1024)[:, None] % 32
    kind = jnp.where((key_col < GRID) & (query_col < GRID), query_col - key_col + GRID - 1, SPAN)
    return jnp.arange(SPAN + 1)[None, :] == kind


def spread_table(table_heads):
    heads = table_heads.shape[0]
    body = table_heads[:, : SPAN * SPAN].reshape(heads, SPAN, SPAN)
    last = jnp.broadcast_to(table_heads[:, NB - 1][:, None, None], (heads, SPAN, 1))
    ext = jnp.concatenate([body, last], axis=2).reshape(heads * SPAN, SPAN + 1)
    full = dot(ext, column_classes().astype(BF), 1, 1)
    full = full.reshape(heads, SPAN, 32, 32).transpose(0, 2, 1, 3).reshape(heads, 32, SPAN * 32)
    return jnp.pad(full, ((0, 0), (0, 0), (0, EW - SPAN * 32)))


def gather_table_grad(acc):
    heads = acc.shape[0]
    pairs = acc[:, :, : SPAN * 32].reshape(heads, 32, SPAN, 32).transpose(0, 2, 1, 3)
    sums = lax.dot_general(
        pairs.reshape(heads * SPAN, 1024),
        column_classes().astype(F32),
        (((1,), (0,)), ((), ())),
        precision=lax.Precision.HIGHEST,
        preferred_element_type=F32,
    ).reshape(heads, SPAN, SPAN + 1)
    body = sums[:, :, :SPAN].reshape(heads, SPAN * SPAN)
    last = jnp.sum(sums[:, :, SPAN], axis=1, keepdims=True)
    gap = jnp.zeros((heads, NB - 1 - SPAN * SPAN), F32)
    return jnp.concatenate([body, gap, last], axis=1).T


def make_local(mesh):
    pairs = [(0, 1), (1, 0)]
    world = mesh.size

    def swap(value):
        return lax.ppermute(value, "img", pairs)

    def local(inputs, flat_params, bias_table, bucket_index, valid_mask, cotangent):
        rows = inputs.shape[1]
        me = lax.axis_index("img")
        stream = inputs[0]
        grad_out = cotangent[0]
        grad_out_b = grad_out.astype(BF)

        table_full = lax.all_gather(bias_table, ("img", "dp"), axis=0, tiled=True)
        flat_full = lax.all_gather(flat_params, ("img", "dp"), axis=0, tiled=True)

        place = slot_places(bucket_index)
        iota = jnp.arange(LP)[:, None]
        here = (place[None, :] == iota)
        valid = valid_mask[0].astype(F32)
        pen = jnp.sum(jnp.where(here, -PENALTY * (1.0 - valid)[None, :], 0.0), axis=1)
        pen = jnp.where(jnp.any(here, axis=1), pen, ABSENT)
        pen = jnp.broadcast_to(pen[:, None], (LP, 128))
        own_place = lax.dynamic_slice_in_dim(place, me * rows, rows, 0)
        far_place = lax.dynamic_slice_in_dim(place, (1 - me) * rows, rows, 0)
        perm_own = (own_place[None, :] == iota).astype(BF)
        perm_far = (far_place[None, :] == iota).astype(BF)

        own_table = lax.dynamic_slice_in_dim(table_full, me * HL, HL, 1)
        bias = spread_table(own_table.T)

        vec = flat_full[D_END : D_END + VECTORS].astype(F32)
        n1_gain, n1_shift, b_query, b_value, b_out, n2_gain, n2_shift, b_down = (
            vec[i * D : (i + 1) * D] for i in range(8)
        )
        b_up = jnp.pad(vec[8 * D :], (0, FFP - FF)).reshape(1, FFP)
        w_qkv = flat_full[:Q_END].reshape(D, 3 * D)
        half = D // 2
        w_half = jnp.concatenate(
            [lax.dynamic_slice_in_dim(w_qkv, i * D + me * half, half, 1) for i in range(3)], axis=1
        )
        w_out = flat_full[Q_END:O_END].reshape(D, D)
        w_up = jnp.pad(flat_full[O_END:U_END].reshape(D, FF), ((0, 0), (0, FFP - FF)))
        w_down = jnp.pad(flat_full[U_END:D_END].reshape(FF, D), ((0, FFP - FF), (0, 0)))
        own_bias = jnp.concatenate(
            [
                lax.dynamic_slice_in_dim(b_query, me * half, half, 0),
                jnp.zeros((half,), F32),
                lax.dynamic_slice_in_dim(b_value, me * half, half, 0),
            ]
        )

        attn_full, normed1, inv_std1 = layer_norm(stream, n1_gain, n1_shift)
        attn_in = attn_full.astype(BF)
        attn_far = swap(attn_in)
        x_grid = (dot(perm_own, attn_in, 1, 0) + dot(perm_far, attn_far, 1, 0)).astype(BF)
        qkv = (dot(w_half, x_grid, 0, 1) + own_bias[:, None]).astype(BF).reshape(3, HL, DH, LP)
        mixed_t, log_norm = run_forward(qkv, bias, pen)
        mixed_t = mixed_t.reshape(half, LP)
        mixed_far = swap(dot(perm_far, mixed_t, 0, 1).astype(BF))
        mixed_own = dot(perm_own, mixed_t, 0, 1).astype(BF)
        mixed = jnp.where(
            me == 0,
            jnp.concatenate([mixed_own, mixed_far], axis=1),
            jnp.concatenate([mixed_far, mixed_own], axis=1),
        )
        resid = stream + dot(mixed, w_out, 1, 0) + b_out
        mlp_full, normed2, inv_std2 = layer_norm(resid, n2_gain, n2_shift)
        mlp_in = mlp_full.astype(BF)
        mlp_out, g_mlp_in, g_up, g_down, g_b_up = run_mlp(mlp_in, grad_out_b, w_up, w_down, b_up)
        output = resid + mlp_out + b_down
        g_b_down = jnp.sum(grad_out, axis=0)
        resid_part, g_n2_gain, g_n2_shift = norm_back(g_mlp_in, normed2, inv_std2, n2_gain)
        grad_resid = grad_out + resid_part
        grad_resid_b = grad_resid.astype(BF)
        g_out = dot(mixed, grad_resid_b, 0, 0).astype(BF)
        g_b_out = jnp.sum(grad_resid, axis=0)
        w_out_own = lax.dynamic_slice_in_dim(w_out, me * half, half, 0)
        w_out_far = lax.dynamic_slice_in_dim(w_out, (1 - me) * half, half, 0)
        d_far = swap(dot(w_out_far, grad_resid_b, 1, 1).astype(BF))
        d_own = dot(w_out_own, grad_resid_b, 1, 1).astype(BF)
        d_mixed = (dot(d_own, perm_own, 1, 1) + dot(d_far, perm_far, 1, 1)).astype(BF)
        grads, acc, sums = run_backward(qkv, d_mixed.reshape(HL, DH, LP), bias, pen, log_norm)
        grads = grads.reshape(3 * half, LP)
        g_half = dot(x_grid, grads, 0, 1).astype(BF)
        grads_far = dot(grads, perm_far, 1, 0).astype(BF)
        back_far = swap(dot(grads_far, w_half, 0, 1).astype(BF))
        grads_own = dot(grads, perm_own, 1, 0).astype(BF)
        g_attn_in = dot(grads_own, w_half, 0, 1) + back_far.astype(F32)
        input_part, g_n1_gain, g_n1_shift = norm_back(g_attn_in, normed1, inv_std1, n1_gain)
        grad_in = grad_resid + input_part

        g_wide = jnp.zeros((D, 3, 2, half), BF)
        g_wide = lax.dynamic_update_slice(g_wide, g_half.reshape(D, 3, 1, half), (0, 0, me, 0))
        flat_grad = jnp.concatenate(
            [
                g_wide.reshape(-1),
                g_out.reshape(-1),
                g_up[:, :FF].reshape(-1),
                g_down[:FF].reshape(-1),
                jnp.zeros((PARAMS_PAD - D_END,), BF),
            ]
        )
        zeros = jnp.zeros((D,), F32)
        g_b_query = lax.dynamic_update_slice(zeros, sums[0, :, :, 0].reshape(-1), (me * half,))
        g_b_value = lax.dynamic_update_slice(zeros, sums[1, :, :, 0].reshape(-1), (me * half,))
        vector_grad = jnp.concatenate(
            [
                g_n1_gain, g_n1_shift, g_b_query, g_b_value, g_b_out, g_n2_gain, g_n2_shift,
                g_b_down, g_b_up[0, :FF], jnp.zeros((VEC_PAD - VECTORS,), F32),
            ]
        )
        table_grad = lax.dynamic_update_slice(
            jnp.zeros((NB, H), F32), gather_table_grad(acc), (0, me * HL)
        )
        small = jnp.concatenate(
            [vector_grad.reshape(world, -1), table_grad.reshape(world, -1)], axis=1
        )
        owned_small = lax.psum_scatter(small, ("img", "dp"), scatter_dimension=0, tiled=True)[0]
        owned_flat = lax.psum_scatter(flat_grad, ("img", "dp"), scatter_dimension=0, tiled=True)
        own_vec = VEC_PAD // world
        return (
            output[None],
            grad_in[None],
            owned_flat.astype(F32),
            owned_small[:own_vec],
            owned_small[own_vec:].reshape(NB // world, H),
        )

    return local


def solution(mesh):
    placed = (
        P("dp", "img", None),
        P(("img", "dp")),
        P(("img", "dp"), None),
        P(),
        P("dp", None),
        P("dp", "img", None),
    )
    return jax.shard_map(
        make_local(mesh),
        mesh=mesh,
        in_specs=placed,
        out_specs=(
            P("dp", "img", None),
            P("dp", "img", None),
            P(("img", "dp")),
            P(("img", "dp")),
            P(("img", "dp"), None),
        ),
        check_vma=False,
    )
```

```python
import math

import jax
import jax.numpy as jnp
from jax import lax
from jax.experimental import pallas as pl
from jax.experimental.pallas import tpu as pltpu
from jax.sharding import PartitionSpec as P

D = 1152
FF = 4304
FFP = 4352
H = 16
HL = 8
DH = 72
SEQ = 768
GRID = 27
SPAN = 53
NB = 2816
PARAMS_PAD = 15253504
VEC_PAD = 16384
EPS = 1e-06
PENALTY = 30000.0
ABSENT = -1e30
GELU_C = math.sqrt(2.0 / math.pi)
GELU_K = 0.044715
SCALE = DH ** (-0.5)

LP = 896
EW = 1792
BF = jnp.bfloat16
F32 = jnp.float32

Q_END = 3 * D * D
O_END = Q_END + D * D
U_END = O_END + D * FF
D_END = U_END + FF * D
VECTORS = 8 * D + FF


def dot(a, b, ca, cb):
    return lax.dot_general(a, b, (((ca,), (cb,)), ((), ())), preferred_element_type=F32)


def offset_of(key_row):
    lead = 26 - key_row
    return lead % 4, (lead // 4) * 128


def wide(column):
    return jnp.concatenate([column] * (LP // 128), axis=1)


def shift_bias(e_ref, e4):
    bias = e_ref[0]
    e4[0] = bias
    for m in range(1, 4):
        e4[m] = pltpu.roll(bias, EW - 32 * m, 1)


def attend_forward(q_ref, k_ref, v_ref, e_ref, pen_ref, out_ref, norm_ref, e4, s_scr, p_scr):
    shift_bias(e_ref, e4)
    q = q_ref[0, 0]
    k = k_ref[0, 0]
    top = jnp.full((32, LP), -jnp.inf, F32)
    for kb in range(7):
        s = dot(k[:, kb * 128 : (kb + 1) * 128], q, 0, 0)
        for sub in range(4):
            row = kb * 4 + sub
            lo = row * 32
            part = s[sub * 32 : sub * 32 + 32] * SCALE
            if row < GRID:
                m, base = offset_of(row)
                part = part + e4[m, :, base : base + LP]
            part = part + wide(pen_ref[lo : lo + 32])
            s_scr[lo : lo + 32] = part
            top = jnp.maximum(top, part)
    row_max = jnp.max(top, axis=0, keepdims=True)
    total = jnp.zeros((32, LP), F32)
    for row in range(28):
        lo = row * 32
        p = jnp.exp(s_scr[lo : lo + 32] - row_max)
        total = total + p
        p_scr[lo : lo + 32] = p.astype(BF)
    row_total = jnp.sum(total, axis=0, keepdims=True)
    mixed = dot(v_ref[0, 0], p_scr[...], 1, 0)
    out_ref[0] = (mixed / row_total).astype(BF)
    norm_ref[0] = row_max + jnp.log(row_total)


def attend_backward(
    q_ref, k_ref, v_ref, do_ref, e_ref, pen_ref, norm_ref,
    grad_ref, acc_ref, sums_ref,
    e4, p_scr, g_scr, pb_scr, gb_scr, acc,
):
    shift_bias(e_ref, e4)
    q = q_ref[0, 0]
    k = k_ref[0, 0]
    v = v_ref[0, 0]
    do = do_ref[0]
    log_norm = norm_ref[0]
    along = jnp.zeros((32, LP), F32)
    for kb in range(7):
        cols = slice(kb * 128, (kb + 1) * 128)
        s = dot(k[:, cols], q, 0, 0)
        g = dot(v[:, cols], do, 0, 0)
        for sub in range(4):
            row = kb * 4 + sub
            lo = row * 32
            part = s[sub * 32 : sub * 32 + 32] * SCALE
            if row < GRID:
                m, base = offset_of(row)
                part = part + e4[m, :, base : base + LP]
            part = part + wide(pen_ref[lo : lo + 32])
            p = jnp.exp(part - log_norm)
            g_part = g[sub * 32 : sub * 32 + 32]
            along = along + p * g_part
            p_scr[lo : lo + 32] = p
            g_scr[lo : lo + 32] = g_part
            pb_scr[lo : lo + 32] = p.astype(BF)
    row_dot = jnp.sum(along, axis=0, keepdims=True)
    acc[...] = jnp.zeros_like(acc)
    for row in range(28):
        lo = row * 32
        ds = p_scr[lo : lo + 32] * (g_scr[lo : lo + 32] - row_dot)
        if row < GRID:
            m, base = offset_of(row)
            acc[m, :, base : base + LP] += ds
        gb_scr[lo : lo + 32] = ds.astype(BF)
    total = acc[0]
    for m in range(1, 4):
        total = total + pltpu.roll(acc[m], 32 * m, 1)
    acc_ref[0] = total
    gb = gb_scr[...]
    dq = dot(k, gb, 1, 0) * SCALE
    dk = dot(q, gb, 1, 1) * SCALE
    dv = dot(do, pb_scr[...], 1, 1)
    grad_ref[0, 0] = dq.astype(BF)
    grad_ref[1, 0] = dk.astype(BF)
    grad_ref[2, 0] = dv.astype(BF)
    sums_ref[0, 0] = jnp.broadcast_to(jnp.sum(dq, axis=1, keepdims=True), (DH, 128))
    sums_ref[1, 0] = jnp.broadcast_to(jnp.sum(dv, axis=1, keepdims=True), (DH, 128))


def head_block(which):
    return pl.BlockSpec((1, 1, DH, LP), lambda h: (which, h, 0, 0))


def run_forward(qkv, bias, pen):
    return pl.pallas_call(
        attend_forward,
        grid=(HL,),
        in_specs=[
            head_block(0),
            head_block(1),
            head_block(2),
            pl.BlockSpec((1, 32, EW), lambda h: (h, 0, 0)),
            pl.BlockSpec((LP, 128), lambda h: (0, 0)),
        ],
        out_specs=[
            pl.BlockSpec((1, DH, LP), lambda h: (h, 0, 0)),
            pl.BlockSpec((1, 1, LP), lambda h: (h, 0, 0)),
        ],
        out_shape=[
            jax.ShapeDtypeStruct((HL, DH, LP), BF),
            jax.ShapeDtypeStruct((HL, 1, LP), F32),
        ],
        scratch_shapes=[
            pltpu.VMEM((4, 32, EW), F32),
            pltpu.VMEM((LP, LP), F32),
            pltpu.VMEM((LP, LP), BF),
        ],
        compiler_params=pltpu.CompilerParams(vmem_limit_bytes=48 * 2**20),
        cost_estimate=pl.CostEstimate(
            flops=HL * 4 * LP * LP * 128, bytes_accessed=8 * 2**20, transcendentals=HL * LP * LP
        ),
        name="attend_forward",
    )(qkv, qkv, qkv, bias, pen)


def run_backward(qkv, d_mixed, bias, pen, log_norm):
    return pl.pallas_call(
        attend_backward,
        grid=(HL,),
        in_specs=[
            head_block(0),
            head_block(1),
            head_block(2),
            pl.BlockSpec((1, DH, LP), lambda h: (h, 0, 0)),
            pl.BlockSpec((1, 32, EW), lambda h: (h, 0, 0)),
            pl.BlockSpec((LP, 128), lambda h: (0, 0)),
            pl.BlockSpec((1, 1, LP), lambda h: (h, 0, 0)),
        ],
        out_specs=[
            pl.BlockSpec((3, 1, DH, LP), lambda h: (0, h, 0, 0)),
            pl.BlockSpec((1, 32, EW), lambda h: (h, 0, 0)),
            pl.BlockSpec((2, 1, DH, 128), lambda h: (0, h, 0, 0)),
        ],
        out_shape=[
            jax.ShapeDtypeStruct((3, HL, DH, LP), BF),
            jax.ShapeDtypeStruct((HL, 32, EW), F32),
            jax.ShapeDtypeStruct((2, HL, DH, 128), F32),
        ],
        scratch_shapes=[
            pltpu.VMEM((4, 32, EW), F32),
            pltpu.VMEM((LP, LP), F32),
            pltpu.VMEM((LP, LP), F32),
            pltpu.VMEM((LP, LP), BF),
            pltpu.VMEM((LP, LP), BF),
            pltpu.VMEM((4, 32, EW), F32),
        ],
        compiler_params=pltpu.CompilerParams(vmem_limit_bytes=48 * 2**20),
        cost_estimate=pl.CostEstimate(
            flops=HL * 10 * LP * LP * 128, bytes_accessed=16 * 2**20, transcendentals=HL * LP * LP
        ),
        name="attend_backward",
    )(qkv, qkv, qkv, d_mixed, bias, pen, log_norm)


FB = 256


def mlp_body(
    x_ref, xt_ref, go_ref, up_ref, down_ref, bias_ref,
    out_ref, gx_ref, g_up_ref, g_down_ref, g_bias_ref,
):
    step = pl.program_id(0)

    @pl.when(step == 0)
    def _():
        out_ref[...] = jnp.zeros_like(out_ref)
        gx_ref[...] = jnp.zeros_like(gx_ref)

    go = go_ref[...]
    up = up_ref[...]
    down = down_ref[...]
    pre = dot(x_ref[...], up, 1, 0) + bias_ref[...]
    square = pre * pre
    t = jnp.tanh(GELU_C * (pre + GELU_K * (square * pre)))
    half = 0.5 * (1.0 + t)
    hidden = (pre * half).astype(BF)
    slope = half + 0.5 * pre * (1.0 - t * t) * (GELU_C * (1.0 + 3.0 * GELU_K * square))
    out_ref[...] += dot(hidden, down, 1, 0)
    g_down_ref[...] = dot(hidden, go, 0, 0).astype(BF)
    grad_pre = dot(go, down, 1, 1) * slope
    g_bias_ref[...] = jnp.sum(grad_pre, axis=0, keepdims=True)
    grad_pre_b = grad_pre.astype(BF)
    g_up_ref[...] = dot(xt_ref[...], grad_pre_b, 1, 0).astype(BF)
    gx_ref[...] += dot(grad_pre_b, up, 1, 1)


def run_mlp(x, grad_out, w_up, w_down, bias_up):
    rows = x.shape[0]
    whole = lambda shape: pl.BlockSpec(shape, lambda j: (0, 0))
    return pl.pallas_call(
        mlp_body,
        grid=(FFP // FB,),
        in_specs=[
            whole((rows, D)),
            whole((D, rows)),
            whole((rows, D)),
            pl.BlockSpec((D, FB), lambda j: (0, j)),
            pl.BlockSpec((FB, D), lambda j: (j, 0)),
            pl.BlockSpec((1, FB), lambda j: (0, j)),
        ],
        out_specs=[
            whole((rows, D)),
            whole((rows, D)),
            pl.BlockSpec((D, FB), lambda j: (0, j)),
            pl.BlockSpec((FB, D), lambda j: (j, 0)),
            pl.BlockSpec((1, FB), lambda j: (0, j)),
        ],
        out_shape=[
            jax.ShapeDtypeStruct((rows, D), F32),
            jax.ShapeDtypeStruct((rows, D), F32),
            jax.ShapeDtypeStruct((D, FFP), BF),
            jax.ShapeDtypeStruct((FFP, D), BF),
            jax.ShapeDtypeStruct((1, FFP), F32),
        ],
        compiler_params=pltpu.CompilerParams(vmem_limit_bytes=48 * 2**20),
        cost_estimate=pl.CostEstimate(
            flops=12 * rows * D * FFP, bytes_accessed=50 * 2**20, transcendentals=rows * FFP
        ),
        name="mlp_both_ways",
    )(x, x.T, grad_out, w_up, w_down, bias_up)


def layer_norm(stream, gain, shift):
    centered = stream - jnp.mean(stream, axis=-1, keepdims=True)
    inv_std = lax.rsqrt(jnp.mean(centered * centered, axis=-1, keepdims=True) + EPS)
    normed = centered * inv_std
    return (normed * gain + shift, normed, inv_std)


def norm_back(grad_out, normed, inv_std, gain):
    grad_normed = grad_out * gain
    grad_in = inv_std * (
        grad_normed
        - jnp.mean(grad_normed, axis=-1, keepdims=True)
        - normed * jnp.mean(grad_normed * normed, axis=-1, keepdims=True)
    )
    return (grad_in, jnp.sum(grad_out * normed, axis=0), jnp.sum(grad_out, axis=0))


def slot_places(bucket_index):
    real = bucket_index < SPAN * SPAN
    row = jnp.max(jnp.where(real, bucket_index // SPAN, -1), axis=1) - (GRID - 1)
    col = jnp.max(jnp.where(real, bucket_index % SPAN, -1), axis=1) - (GRID - 1)
    empty = row < 0
    earlier = jnp.arange(SEQ)[:, None] > jnp.arange(SEQ)[None, :]
    rank = jnp.sum(jnp.where(earlier & empty[None, :], 1, 0), axis=1)
    spare = (rank // 5) * 32 + GRID + rank % 5
    return jnp.where(empty, spare, row * 32 + col)


def column_classes():
    key_col = jnp.arange(1024)[:, None] // 32
    query_col = jnp.arange(1024)[:, None] % 32
    kind = jnp.where((key_col < GRID) & (query_col < GRID), query_col - key_col + GRID - 1, SPAN)
    return jnp.arange(SPAN + 1)[None, :] == kind


def spread_table(table_heads):
    heads = table_heads.shape[0]
    body = table_heads[:, : SPAN * SPAN].reshape(heads, SPAN, SPAN)
    last = jnp.broadcast_to(table_heads[:, NB - 1][:, None, None], (heads, SPAN, 1))
    ext = jnp.concatenate([body, last], axis=2).reshape(heads * SPAN, SPAN + 1)
    full = dot(ext, column_classes().astype(BF), 1, 1)
    full = full.reshape(heads, SPAN, 32, 32).transpose(0, 2, 1, 3).reshape(heads, 32, SPAN * 32)
    return jnp.pad(full, ((0, 0), (0, 0), (0, EW - SPAN * 32)))


def gather_table_grad(acc):
    heads = acc.shape[0]
    pairs = acc[:, :, : SPAN * 32].reshape(heads, 32, SPAN, 32).transpose(0, 2, 1, 3)
    sums = lax.dot_general(
        pairs.reshape(heads * SPAN, 1024),
        column_classes().astype(F32),
        (((1,), (0,)), ((), ())),
        precision=lax.Precision.HIGHEST,
        preferred_element_type=F32,
    ).reshape(heads, SPAN, SPAN + 1)
    body = sums[:, :, :SPAN].reshape(heads, SPAN * SPAN)
    last = jnp.sum(sums[:, :, SPAN], axis=1, keepdims=True)
    gap = jnp.zeros((heads, NB - 1 - SPAN * SPAN), F32)
    return jnp.concatenate([body, gap, last], axis=1).T


TQ, TO, TU, TD = 0, 3888, 5184, 10026
TEND = 14868
TILES = 14896
GRAD_TILES = TD + 17 * 288

def tile_spec(count, start):
    return pl.BlockSpec((pl.Element(count), pl.Element(8), pl.Element(128)), lambda g, *_: (start + g * count, 0, 0))

def lanes(rows):
    return lax.broadcasted_iota(jnp.int32, (rows, 128), 1)

def load_flat(ref, scr):
    n = ref.shape[0]
    scr[...] = ref[...].astype(F32).reshape(n * 8, 128)

def store_flat(ref, scr):
    n = ref.shape[0]
    ref[...] = scr[...].reshape(n, 8, 128).astype(BF)

def qkv_in_body(me_ref, ref, out, scr):
    load_flat(ref, scr)
    rows = out.shape[0]
    lane = lanes(rows)
    def go(me):
        def half(u):
            v = 18 * (u // 9) + 9 * me + u % 9
            x = scr[pl.ds(v // 2, rows, stride=27), :]
            return x if v % 2 == u % 2 else pltpu.roll(x, 64, 1)
        for J in range(13):
            out[:, J * 128:(J + 1) * 128] = jnp.where(lane < 64, half(2 * J), half(2 * J + 1)).astype(BF)
        out[:, 13 * 128:] = half(26)[:, :64].astype(BF)
    pl.when(me_ref[0] == 0)(lambda: go(0))
    pl.when(me_ref[0] == 1)(lambda: go(1))

def qkv_out_body(me_ref, x_ref, *rest):
    ref, scr = rest[-2:]
    rows = x_ref.shape[0]
    lane = lanes(rows)
    def go(me):
        def half(v, side):
            i, w = v // 18, v % 18
            if w // 9 != me:
                return jnp.zeros((rows, 128), F32)
            u = 9 * i + w % 9
            if u == 26:
                x = jnp.concatenate([x_ref[:, 13 * 128:], x_ref[:, 13 * 128:]], axis=1).astype(F32)
                return x
            x = x_ref[:, (u // 2) * 128:(u // 2) * 128 + 128].astype(F32)
            return x if u % 2 == side else pltpu.roll(x, 64, 1)
        for J in range(27):
            scr[pl.ds(J, rows, stride=27), :] = jnp.where(lane < 64, half(2 * J, 0), half(2 * J + 1, 1))
    pl.when(me_ref[0] == 0)(lambda: go(0))
    pl.when(me_ref[0] == 1)(lambda: go(1))
    store_flat(ref, scr)

def plain_in_body(last, ref, out, scr):
    load_flat(ref, scr)
    rows = out.shape[0]
    def go(shift, count):
        for j in range(9):
            x = scr[pl.ds(shift + j, count, stride=9), :].astype(BF)
            if count < rows:
                x = jnp.concatenate([x, jnp.zeros((rows - count, 128), BF)], axis=0)
            out[:, j * 128:(j + 1) * 128] = x
    if last is None:
        go(0, rows)
    else:
        g = pl.program_id(0)
        pl.when(g < pl.num_programs(0) - 1)(lambda: go(0, rows))
        pl.when(g == pl.num_programs(0) - 1)(lambda: go(*last))

def plain_out_body(x_ref, *rest):
    ref, scr = rest[-2:]
    rows = x_ref.shape[0]
    for j in range(9):
        scr[pl.ds(j, rows, stride=9), :] = x_ref[:, j * 128:(j + 1) * 128].astype(F32)
    store_flat(ref, scr)

def up_in_body(ref, out, scr, wide):
    load_flat(ref, scr)
    lane = lanes(8)
    for p in range(8):
        k0, o = divmod(FF * p, 128)
        prev = None
        for j in range(35):
            if k0 + j < 269:
                x = scr[pl.ds(k0 + j, 8, stride=269), :]
                if o:
                    x = pltpu.roll(x, 128 - o, 1)
            if j > 0:
                blk = prev if o == 0 else jnp.where(lane < 128 - o, prev, x)
                wide[j - 1, pl.ds(p, 8, stride=8), :] = blk
            prev = x
    for j in range(34):
        out[:, j * 128:(j + 1) * 128] = wide[j].astype(BF)

def up_out_body(x_ref, *rest):
    ref, scr, wide = rest[-3:]
    for j in range(34):
        wide[j] = x_ref[:, j * 128:(j + 1) * 128].astype(F32)
    lane = lanes(8)
    carry = None
    for p in range(8):
        k0, o = divmod(FF * p, 128)
        k1, e = divmod(FF * (p + 1), 128)
        prev = carry
        for j in range(k1 - k0 + 1):
            if j < 34:
                x = wide[j, pl.ds(p, 8, stride=8), :]
                if o:
                    x = pltpu.roll(x, o, 1)
            cur = x if o == 0 else jnp.where(lane < o, prev, x)
            if k0 + j < k1:
                scr[pl.ds(k0 + j, 8, stride=269), :] = cur
            else:
                carry = cur
            prev = x
    store_flat(ref, scr)

PARAMS = pltpu.CompilerParams(vmem_limit_bytes=40 * 2**20)

def scr_of(count):
    return pltpu.VMEM((count * 8, 128), F32)

def qkv_in(flat, me):
    return pl.pallas_call(
        qkv_in_body,
        grid_spec=pltpu.PrefetchScalarGridSpec(num_scalar_prefetch=1, grid=(12,),
            in_specs=[tile_spec(324, TQ)], out_specs=pl.BlockSpec((96, 1728), lambda g, *_: (g, 0)),
            scratch_shapes=[scr_of(324)]),
        out_shape=jax.ShapeDtypeStruct((D, 1728), BF), compiler_params=PARAMS, name="qkv_in")(me, flat)

def out_in(flat):
    return pl.pallas_call(
        lambda *r: plain_in_body(None, *r), grid=(9,), in_specs=[tile_spec(144, TO)],
        out_specs=pl.BlockSpec((128, D), lambda g: (g, 0)), scratch_shapes=[scr_of(144)],
        out_shape=jax.ShapeDtypeStruct((D, D), BF), compiler_params=PARAMS, name="out_in")(flat)

def up_in(flat):
    return pl.pallas_call(
        up_in_body, grid=(18,), in_specs=[tile_spec(269, TU)],
        out_specs=pl.BlockSpec((64, FFP), lambda g: (g, 0)), scratch_shapes=[scr_of(269), pltpu.VMEM((34, 64, 128), F32)],
        out_shape=jax.ShapeDtypeStruct((D, FFP), BF), compiler_params=PARAMS, name="up_in")(flat)

def down_in(flat):
    spec = pl.BlockSpec((pl.Element(288), pl.Element(8), pl.Element(128)), lambda g: (jnp.minimum(TD + g * 288, TILES - 288), 0, 0))
    return pl.pallas_call(
        lambda *r: plain_in_body((208, 208), *r), grid=(17,), in_specs=[spec],
        out_specs=pl.BlockSpec((256, D), lambda g: (g, 0)), scratch_shapes=[scr_of(288)],
        out_shape=jax.ShapeDtypeStruct((FFP, D), BF), compiler_params=PARAMS, name="down_in")(flat)

GRAD = jax.ShapeDtypeStruct((GRAD_TILES, 8, 128), BF)
ANY = pl.BlockSpec(memory_space=pl.ANY)

def down_out(x):
    return pl.pallas_call(
        plain_out_body, grid=(17,), in_specs=[pl.BlockSpec((256, D), lambda g: (g, 0))],
        out_specs=tile_spec(288, TD), scratch_shapes=[scr_of(288)],
        out_shape=GRAD, compiler_params=PARAMS, name="down_out")(x)

def up_out(x, flat):
    return pl.pallas_call(
        up_out_body, grid=(18,), in_specs=[pl.BlockSpec((64, FFP), lambda g: (g, 0)), ANY],
        out_specs=tile_spec(269, TU), scratch_shapes=[scr_of(269), pltpu.VMEM((34, 64, 128), F32)],
        input_output_aliases={1: 0},
        out_shape=GRAD, compiler_params=PARAMS, name="up_out")(x, flat)

def out_out(x, flat):
    return pl.pallas_call(
        plain_out_body, grid=(9,), in_specs=[pl.BlockSpec((128, D), lambda g: (g, 0)), ANY],
        out_specs=tile_spec(144, TO), scratch_shapes=[scr_of(144)], input_output_aliases={1: 0},
        out_shape=GRAD, compiler_params=PARAMS, name="out_out")(x, flat)

def qkv_out(x, flat, me):
    return pl.pallas_call(
        qkv_out_body,
        grid_spec=pltpu.PrefetchScalarGridSpec(num_scalar_prefetch=1, grid=(12,),
            in_specs=[pl.BlockSpec((96, 1728), lambda g, *_: (g, 0)), ANY], out_specs=tile_spec(324, TQ),
            scratch_shapes=[scr_of(324)]),
        input_output_aliases={2: 0},
        out_shape=GRAD, compiler_params=PARAMS, name="qkv_out")(me, x, flat)


TILE = 1024


class Net:
    def __init__(self, mesh):
        self.dp = mesh.shape["dp"]
        self.chips = mesh.size // 2
        half = self.chips // 2
        bits = [1 << i for i in range(half.bit_length() - 1)]
        x, zs, y = bits[0], bits[1:], half
        self.orders = (zs + [x, y], zs + [y, x])
        self.stages = len(self.orders[0])
        self.core_pairs = [(d, d ^ 1) for d in range(mesh.size)]

    def stage_pairs(self, s):
        return [
            (2 * q + c, 2 * (q ^ self.orders[c][s]) + c) for q in range(self.chips) for c in (0, 1)
        ]

    def send(self, value, pairs):
        return lax.ppermute(value, ("img", "dp"), pairs)

    def mask(self, b, c):
        total = 0
        for s in range(self.stages):
            if b >> s & 1:
                total ^= self.orders[c][s]
        return total

    def place(self):
        me = lax.axis_index("img") * self.dp + lax.axis_index("dp")
        return me // 2, me % 2

    def offsets(self, tiles):
        chip, core = self.place()
        masks = jnp.array(
            [[self.mask(b, c) for b in range(self.chips)] for c in (0, 1)], jnp.int32
        )
        step = (tiles - 1) // 2
        own = (chip ^ masks[core]) * tiles + core * step
        far = (chip ^ masks[1 - core]) * tiles + (1 - core) * step
        return own, far


def unfilled(shape):
    return pl.pallas_call(
        lambda ref: None,
        out_specs=pl.BlockSpec(memory_space=pl.ANY),
        out_shape=jax.ShapeDtypeStruct(shape, BF),
        name="unfilled",
    )()


def chip_part(net, shard):
    _, core = net.place()
    length = shard.shape[0]
    gap = -length % TILE
    got = net.send(jnp.where(core == 0, shard[length - gap :], shard[:gap]), net.core_pairs)
    both = jnp.where(core == 0, jnp.concatenate([shard, got]), jnp.concatenate([got, shard]))
    return both.reshape(-1, 8, 128)


def gather_flat(net, shard):
    tiles = 2 * shard.shape[0] // TILE
    own = {0: chip_part(net, shard)}
    far = {}
    own_at, far_at = net.offsets(tiles)
    flat = unfilled((net.chips * tiles, 8, 128))
    for s in range(net.stages):
        for b in range(1 << s):
            own[b + (1 << s)] = net.send(own[b], net.stage_pairs(s))
    for b in range(net.chips):
        far[b] = net.send(own[b], net.core_pairs)
        flat = lax.dynamic_update_slice(flat, own[b], (own_at[b], 0, 0))
        flat = lax.dynamic_update_slice(flat, far[b], (far_at[b], 0, 0))
    return flat


def add(a, b):
    return (a.astype(F32) + b.astype(F32)).astype(BF)


def scatter_flat(net, flat, length):
    tiles = 2 * length // TILE
    half = (tiles + 1) // 2
    own_at, far_at = net.offsets(tiles)
    acc = {}
    for b in reversed(range(net.chips)):
        away = lax.dynamic_slice(flat, (far_at[b], 0, 0), (half, 8, 128))
        came = net.send(away, net.core_pairs)
        acc[b] = add(lax.dynamic_slice(flat, (own_at[b], 0, 0), (half, 8, 128)), came)
    for s in reversed(range(net.stages)):
        for b in reversed(range(1 << s)):
            came = net.send(acc.pop(b + (1 << s)), net.stage_pairs(s))
            acc[b] = add(acc[b], came) if s else acc[b].astype(F32) + came.astype(F32)
    total = acc[0].reshape(-1)
    _, core = net.place()
    return jnp.where(core == 0, total[:length], total[half * TILE - length :])


def gather_table(bias_table, world):
    rows, heads = bias_table.shape
    size = rows * heads
    full = -(-size // TILE) * TILE
    shard = jnp.pad(bias_table.reshape(-1), (0, full - size)).reshape(-1, 8, 128)
    got = lax.all_gather(shard, ("img", "dp"), axis=0, tiled=True)
    return got.reshape(world, full)[:, :size].reshape(world * rows, heads)


def make_local(mesh):
    pairs = [(0, 1), (1, 0)]
    world = mesh.size

    def swap(value):
        return lax.ppermute(value, "img", pairs)

    def local(inputs, flat_params, bias_table, bucket_index, valid_mask, cotangent):
        rows = inputs.shape[1]
        me = lax.axis_index("img")
        stream = inputs[0]
        grad_out = cotangent[0]
        grad_out_b = grad_out.astype(BF)

        shard = flat_params.shape[0]
        paired = (2 * shard) % TILE == 0 and mesh.size & (mesh.size - 1) == 0
        net = Net(mesh) if paired else None
        if paired:
            flat_full = gather_flat(net, flat_params)
        else:
            flat_full = lax.all_gather(flat_params, ("img", "dp"), axis=0, tiled=True)
            flat_full = flat_full.reshape(TILES, 8, 128)
        table_full = gather_table(bias_table, world)

        place = slot_places(bucket_index)
        iota = jnp.arange(LP)[:, None]
        here = (place[None, :] == iota)
        valid = valid_mask[0].astype(F32)
        pen = jnp.sum(jnp.where(here, -PENALTY * (1.0 - valid)[None, :], 0.0), axis=1)
        pen = jnp.where(jnp.any(here, axis=1), pen, ABSENT)
        pen = jnp.broadcast_to(pen[:, None], (LP, 128))
        own_place = lax.dynamic_slice_in_dim(place, me * rows, rows, 0)
        far_place = lax.dynamic_slice_in_dim(place, (1 - me) * rows, rows, 0)
        perm_own = (own_place[None, :] == iota).astype(BF)
        perm_far = (far_place[None, :] == iota).astype(BF)

        own_table = lax.dynamic_slice_in_dim(table_full, me * HL, HL, 1)
        bias = spread_table(own_table.T)

        vec = flat_full[TEND : TEND + 14].reshape(-1)[:VECTORS].astype(F32)
        n1_gain, n1_shift, b_query, b_value, b_out, n2_gain, n2_shift, b_down = (
            vec[i * D : (i + 1) * D] for i in range(8)
        )
        b_up = jnp.pad(vec[8 * D :], (0, FFP - FF)).reshape(1, FFP)
        half = D // 2
        w_half = qkv_in(flat_full, me[None])
        w_out = out_in(flat_full)
        w_up = up_in(flat_full)
        w_down = down_in(flat_full)
        own_bias = jnp.concatenate(
            [
                lax.dynamic_slice_in_dim(b_query, me * half, half, 0),
                jnp.zeros((half,), F32),
                lax.dynamic_slice_in_dim(b_value, me * half, half, 0),
            ]
        )

        attn_full, normed1, inv_std1 = layer_norm(stream, n1_gain, n1_shift)
        attn_in = attn_full.astype(BF)
        attn_far = swap(attn_in)
        x_grid = (dot(perm_own, attn_in, 1, 0) + dot(perm_far, attn_far, 1, 0)).astype(BF)
        qkv = (dot(w_half, x_grid, 0, 1) + own_bias[:, None]).astype(BF).reshape(3, HL, DH, LP)
        mixed_t, log_norm = run_forward(qkv, bias, pen)
        mixed_t = mixed_t.reshape(half, LP)
        mixed_far = swap(dot(perm_far, mixed_t, 0, 1).astype(BF))
        mixed_own = dot(perm_own, mixed_t, 0, 1).astype(BF)
        mixed = jnp.where(
            me == 0,
            jnp.concatenate([mixed_own, mixed_far], axis=1),
            jnp.concatenate([mixed_far, mixed_own], axis=1),
        )
        resid = stream + dot(mixed, w_out, 1, 0) + b_out
        mlp_full, normed2, inv_std2 = layer_norm(resid, n2_gain, n2_shift)
        mlp_in = mlp_full.astype(BF)
        mlp_out, g_mlp_in, g_up, g_down, g_b_up = run_mlp(mlp_in, grad_out_b, w_up, w_down, b_up)
        output = resid + mlp_out + b_down
        g_b_down = jnp.sum(grad_out, axis=0)
        resid_part, g_n2_gain, g_n2_shift = norm_back(g_mlp_in, normed2, inv_std2, n2_gain)
        grad_resid = grad_out + resid_part
        grad_resid_b = grad_resid.astype(BF)
        g_out = dot(mixed, grad_resid_b, 0, 0).astype(BF)
        g_b_out = jnp.sum(grad_resid, axis=0)
        w_out_own = lax.dynamic_slice_in_dim(w_out, me * half, half, 0)
        w_out_far = lax.dynamic_slice_in_dim(w_out, (1 - me) * half, half, 0)
        d_far = swap(dot(w_out_far, grad_resid_b, 1, 1).astype(BF))
        d_own = dot(w_out_own, grad_resid_b, 1, 1).astype(BF)
        d_mixed = (dot(d_own, perm_own, 1, 1) + dot(d_far, perm_far, 1, 1)).astype(BF)
        grads, acc, sums = run_backward(qkv, d_mixed.reshape(HL, DH, LP), bias, pen, log_norm)
        grads = grads.reshape(3 * half, LP)
        g_half = dot(x_grid, grads, 0, 1).astype(BF)
        grads_far = dot(grads, perm_far, 1, 0).astype(BF)
        back_far = swap(dot(grads_far, w_half, 0, 1).astype(BF))
        grads_own = dot(grads, perm_own, 1, 0).astype(BF)
        g_attn_in = dot(grads_own, w_half, 0, 1) + back_far.astype(F32)
        input_part, g_n1_gain, g_n1_shift = norm_back(g_attn_in, normed1, inv_std1, n1_gain)
        grad_in = grad_resid + input_part

        flat_grad = down_out(g_down)
        flat_grad = up_out(g_up, flat_grad)
        flat_grad = out_out(g_out, flat_grad)
        flat_grad = qkv_out(g_half, flat_grad, me[None])
        zeros = jnp.zeros((D,), F32)
        g_b_query = lax.dynamic_update_slice(zeros, sums[0, :, :, 0].reshape(-1), (me * half,))
        g_b_value = lax.dynamic_update_slice(zeros, sums[1, :, :, 0].reshape(-1), (me * half,))
        vector_grad = jnp.concatenate(
            [
                g_n1_gain, g_n1_shift, g_b_query, g_b_value, g_b_out, g_n2_gain, g_n2_shift,
                g_b_down, g_b_up[0, :FF], jnp.zeros((VEC_PAD - VECTORS,), F32),
            ]
        )
        table_grad = lax.dynamic_update_slice(
            jnp.zeros((NB, H), F32), gather_table_grad(acc), (0, me * HL)
        )
        small = jnp.concatenate(
            [vector_grad.reshape(world, -1), table_grad.reshape(world, -1)], axis=1
        )
        owned_small = lax.psum_scatter(small, ("img", "dp"), scatter_dimension=0, tiled=True)[0]
        if paired:
            owned_flat = scatter_flat(net, flat_grad, shard)
        else:
            owned_flat = lax.psum_scatter(
                flat_grad[:TILES].reshape(-1), ("img", "dp"), scatter_dimension=0, tiled=True
            ).astype(F32)
        number = me * mesh.shape["dp"] + lax.axis_index("dp")
        spot = jnp.arange(shard) + number * shard
        owned_flat = jnp.where(spot < D_END, owned_flat, 0.0)
        own_vec = VEC_PAD // world
        return (
            output[None],
            grad_in[None],
            owned_flat,
            owned_small[:own_vec],
            owned_small[own_vec:].reshape(NB // world, H),
        )

    return local


def solution(mesh):
    placed = (
        P("dp", "img", None),
        P(("img", "dp")),
        P(("img", "dp"), None),
        P(),
        P("dp", None),
        P("dp", "img", None),
    )
    return jax.shard_map(
        make_local(mesh),
        mesh=mesh,
        in_specs=placed,
        out_specs=(
            P("dp", "img", None),
            P("dp", "img", None),
            P(("img", "dp")),
            P(("img", "dp")),
            P(("img", "dp"), None),
        ),
        check_vma=False,
    )
```
